512 devices in a mesh: dp: 64 (over z_hi, y, x), fsdp: 8 (over z_lo, core).
Axes of the slice: x: 4, y: 8, z: 8 (z_hi: 2, z_lo: 4; z = z_hi * 4 + z_lo), core: 2. Of those that a mesh axis runs over, the one named last changes fastest.
Arguments:
- activations: bfloat16 [24576, 4096], P('dp', 'fsdp'), may hold values from -16 to 16
- grad_out: bfloat16 [24576, 14336], P('dp', 'fsdp'), may hold values from -0.0234375 to 0.0234375
- projector: bfloat16 [1024, 14336], P('dp', 'fsdp'), may hold values from -0.1875 to 0.1875
- weight: bfloat16 [8, 512, 14336], P(None, 'dp', 'fsdp'), may hold values from -6 to 6
- moment_one_in: float32 [8, 512, 1024], P('fsdp', 'dp'), may hold values from -6 to 6
- moment_two_in: float32 [8, 512, 1024], P('fsdp', 'dp'), may hold values from 0.25 to 4
Outputs:
- new_weight: bfloat16 [8, 512, 14336], P(None, 'dp')
- moment_one: float32 [8, 512, 1024], P('fsdp', 'dp')
- moment_two: float32 [8, 512, 1024], P('fsdp', 'dp')
The draws below stay inside these ranges and needn't reach their ends.
All inputs are finite; a program needn't handle non-finite values.
Results may differ from the reference program's by a relative error of at most 0.003.
Values may be sent and summed in bfloat16 or wider, within the bound.
No kernel may reach another device: no remote copies, remote signals or barrier semaphores. Data moves between devices by JAX's collectives and lax.ppermute only.
A program may use at most 64 MiB of HBM per device.

```python
import math
import jax
import jax.numpy as jnp
from jax import lax

D = 4096
FF = 14336
R = 1024
TOKENS = 24576
BLOCKS = 8
BLK = 512


def raised(entries, stream_key, source, target, parts, factor):
    owner, partner = [(jnp.arange(entries.shape[position]) // (entries.shape[position] // parts)).reshape([-1 if axis == position else 1 for axis in range(entries.ndim)]) for position in (source, target)]
    chosen = jax.random.permutation(stream_key, parts)[partner]
    strong = (owner == chosen) | (owner == (partner + parts // 2) % parts)
    return jnp.where(strong, factor * entries, entries)


def level_of(key, shape, cuts, low, largest):
    loudness, own = 1.0, jax.random.fold_in(key, 6)
    for axis_at, blocks in cuts:
        draws = jnp.exp(jax.random.uniform(jax.random.fold_in(own, axis_at), (blocks,), jnp.float32, low / len(cuts), largest / len(cuts)))
        loudness = loudness * jnp.repeat(draws, shape[axis_at] // blocks).reshape([-1 if axis == axis_at else 1 for axis in range(len(shape))])
    return loudness


def centred(rng, shape, scale, most, cuts=(), kind=jnp.bfloat16):
    drawn = scale * jax.random.normal(rng, shape, jnp.float32)
    if cuts:
        drawn = drawn * level_of(rng, shape, cuts, -0.22, 0.18)
    return jnp.clip(drawn, -most, most).astype(kind)


def heavy_noise(stream_key, shape, width, most, shards, heavy, dtype=jnp.bfloat16):
    drawn = width * jax.random.normal(stream_key, shape, jnp.float32)
    if shards:
        drawn = drawn * level_of(stream_key, shape, shards, -0.22, 0.18)
    return jnp.clip(raised(drawn, jax.random.fold_in(stream_key, 3), *heavy), -most, most).astype(dtype)


def setup_inputs(seed: int = 0) -> dict:
    key_list = jax.random.split(jax.random.key(seed), 7)
    return {
        "activations": heavy_noise(key_list[0], (TOKENS, D), 1.0, 16.0, ((0, 64), (1, 8)), (0, 1, 64, 4.0)),
        "grad_out": centred(key_list[1], (TOKENS, FF), ((R / (FF * TOKENS)) ** 0.5), 0.0234375, ((0, 64), (1, 8))),
        "projector": centred(key_list[2], (R, FF), R ** -0.5, 0.1875, ((0, 64), (1, 8))),
        "weight": centred(key_list[3], (BLOCKS, BLK, FF), 0.5, 6.0, ((1, 64), (2, 8))),
        "moment_one_in": centred(key_list[4], (BLOCKS, BLK, R), 1.0, 6.0, ((0, 8), (1, 64)), jnp.float32),
        "moment_two_in": jnp.clip(jnp.exp(math.log(4.0) - 2.7725887 * jax.random.uniform(key_list[5], (BLOCKS, BLK, R), jnp.float32) ** level_of(key_list[5], (BLOCKS, BLK, R), ((0, 8), (1, 64)), -0.2, 0.2)), 0.25, 4.0),
    }


decay_first = 0.9
decay_second = 0.95
bias_first = 1.0 / (1.0 - 0.9 ** 10)
bias_second = 1.0 / (1.0 - 0.95 ** 10)
step_scale = 0.25
epsilon = 1e-08

def reference(activations, grad_out, projector, weight, moment_one_in, moment_two_in):
    projected = lax.dot_general(grad_out, projector, (((1,), (1,)), ((), ())), preferred_element_type=jnp.float32).astype(jnp.bfloat16)
    low_grad = lax.dot_general(activations, projected, (((0,), (0,)), ((), ())), preferred_element_type=jnp.float32)
    low_grad = low_grad.reshape(moment_one_in.shape)
    moment_one = decay_first * moment_one_in + (1.0 - decay_first) * low_grad
    moment_two = decay_second * moment_two_in + (1.0 - decay_second) * low_grad * low_grad
    direction = (bias_first * moment_one / (jnp.sqrt(bias_second * moment_two) + epsilon)).astype(jnp.bfloat16)
    stacked = direction.reshape(-1, direction.shape[-1])
    update = jnp.dot(stacked, projector, preferred_element_type=jnp.float32)
    new_weight = (weight.astype(jnp.float32) - step_scale * update.reshape(weight.shape)).astype(jnp.bfloat16)
    return (new_weight, moment_one, moment_two)
```

```python
import jax
import jax.numpy as jnp
from jax import lax
from jax.sharding import Mesh, PartitionSpec as P

decay_first = 0.9
decay_second = 0.95
bias_first = 1.0 / (1.0 - 0.9**10)
bias_second = 1.0 / (1.0 - 0.95**10)
step_scale = 0.25
epsilon = 1e-08

fine_axes = ("zh", "y", "x", "zl", "core")
fine_sizes = (2, 8, 4, 4, 2)
dp = ("zh", "y", "x")
rest = ("zh", "y")
fsdp = ("zl", "core")


def gather(block, axes):
    return lax.all_gather(block, axes, axis=0, tiled=True)


def exchange(block, axes):
    return lax.all_to_all(block, axes, 0, 0, tiled=True)


def contract(left, right, dims):
    return lax.dot_general(left, right, (dims, ((), ())), preferred_element_type=jnp.float32)


def summed(pieces):
    return jnp.sum(pieces.astype(jnp.float32), axis=0)


def ranks_by_x(moment):
    rows, ranks = moment.shape
    return moment.reshape(rows, 2, 8, 4, 16).transpose(0, 3, 2, 1, 4).reshape(rows, ranks)


def ranks_in_order(moment):
    rows, ranks = moment.shape
    return moment.reshape(rows, 4, 8, 2, 16).transpose(0, 3, 2, 1, 4).reshape(rows, ranks)


def shards(activations, grad_out, projector, weight, moment_one_in, moment_two_in):
    blocks, rows, ff_local = weight.shape
    rank_total = moment_one_in.shape[2]

    tokens_grad = gather(grad_out, "x")
    quarter = gather(gather(projector, "zh"), "y")
    tokens_act = gather(activations, "x")
    basis = gather(quarter, "x")
    first_in = ranks_by_x(moment_one_in[0])
    second_in = ranks_by_x(moment_two_in[0])

    partial = contract(tokens_grad, quarter, ((1,), (1,))).astype(jnp.bfloat16)
    tokens, ranks = partial.shape
    pieces = exchange(partial.reshape(8, tokens // 8, ranks), fsdp)
    projected = gather(summed(pieces).astype(jnp.bfloat16), fsdp)

    low = contract(tokens_act, projected, ((0,), (0,))).astype(jnp.bfloat16)
    pieces = exchange(low.reshape(16, low.shape[0] // 16, ranks), rest)
    low = summed(pieces)
    low = exchange(low.reshape(4, rows, ranks), "x")
    low_grad = low.transpose(1, 0, 2).reshape(rows, rank_total)

    moment_one = decay_first * first_in + (1.0 - decay_first) * low_grad
    moment_two = decay_second * second_in + (1.0 - decay_second) * low_grad * low_grad
    direction = (bias_first * moment_one / (jnp.sqrt(bias_second * moment_two) + epsilon)).astype(
        jnp.bfloat16
    )
    copies = jnp.broadcast_to(direction[None], (8, rows, rank_total))
    stacked = exchange(copies, fsdp).reshape(blocks * rows, rank_total)

    update = contract(stacked, basis, ((1,), (0,)))
    updated = (weight.astype(jnp.float32) - step_scale * update.reshape(weight.shape)).astype(
        jnp.bfloat16
    )
    column = gather(updated[None], "zl")
    halves = [
        lax.all_gather(column[:, part * 4 : part * 4 + 4], "core", axis=1) for part in range(2)
    ]
    both = jnp.concatenate(halves, axis=2)
    new_weight = both.transpose(2, 3, 0, 1, 4).reshape(blocks, rows, 8 * ff_local)
    return (
        new_weight,
        ranks_in_order(moment_one)[None],
        ranks_in_order(moment_two)[None],
    )


def solution(mesh):
    fine = Mesh(mesh.devices.reshape(fine_sizes), fine_axes)
    in_specs = (
        P(dp, fsdp),
        P(dp, fsdp),
        P(dp, fsdp),
        P(None, dp, fsdp),
        P(fsdp, dp, None),
        P(fsdp, dp, None),
    )
    out_specs = (P(None, dp, None), P(fsdp, dp, None), P(fsdp, dp, None))
    return jax.shard_map(shards, mesh=fine, in_specs=in_specs, out_specs=out_specs, check_vma=False)
```

```python
import jax
import jax.numpy as jnp
from jax import lax
from jax.sharding import Mesh, PartitionSpec as P

decay_first = 0.9
decay_second = 0.95
bias_first = 1.0 / (1.0 - 0.9**10)
bias_second = 1.0 / (1.0 - 0.95**10)
step_scale = 0.25
epsilon = 1e-08

fine_axes = ("zh", "y", "x", "zl", "core")
fine_sizes = (2, 8, 4, 4, 2)
dp = ("zh", "y", "x")
rest = ("zh", "y")
fsdp = ("zl", "core")


def exchange(block, axes):
    return lax.all_to_all(block, axes, 0, 0, tiled=True)


def copies(block, axes):
    return exchange(jnp.broadcast_to(block[None], (lax.axis_size(axes),) + block.shape), axes)


def contract(left, right, dims):
    return lax.dot_general(left, right, (dims, ((), ())), preferred_element_type=jnp.float32)


def summed(pieces):
    return jnp.sum(pieces.astype(jnp.float32), axis=0)


def shift(block, pairs):
    return lax.ppermute(block, "x", [(i, j) for i, j in enumerate(pairs)])


def after(block, *others):
    return lax.optimization_barrier((block,) + others)[0]


partner = (1, 0, 3, 2)
mirror = (3, 2, 1, 0)
quarters = (0, 3, 1, 2)


def ranks_by_half(moment):
    rows, ranks = moment.shape
    parts = moment.reshape(rows, 2, 8, 4, 16).transpose(0, 3, 2, 1, 4)
    return jnp.concatenate([parts[:, q : q + 1] for q in quarters], axis=1).reshape(rows, ranks)


def ranks_in_order(moment):
    rows, ranks = moment.shape
    parts = moment.reshape(rows, 4, 8, 2, 16)
    parts = [parts[:, quarters.index(q)][:, None] for q in range(4)]
    return jnp.concatenate(parts, axis=1).transpose(0, 3, 2, 1, 4).reshape(rows, ranks)


def gather(block, axes):
    return lax.all_gather(block, axes, axis=0, tiled=True)


def shards(activations, grad_out, projector, weight, moment_one_in, moment_two_in):
    blocks, rows, ff_local = weight.shape
    rank_total = moment_one_in.shape[2]
    tokens, features = activations.shape
    groups = lax.axis_size(fsdp)
    place = lax.axis_index("x")
    low_place = place < 2

    grad_pair = shift(grad_out, partner)
    act_pair = shift(activations, partner)
    own = gather(gather(projector, "zh"), "y")
    other = shift(own, mirror)
    ranks = own.shape[0]

    def project(basis):
        parts = [
            contract(part, basis, ((1,), (1,))).astype(jnp.bfloat16)
            for part in (grad_out, grad_pair)
        ]
        return jnp.concatenate(parts).reshape(groups, -1, ranks)

    near = summed(exchange(project(own), fsdp))
    far = summed(exchange(project(after(other, near)), fsdp))
    pair_own = shift(own, partner)
    pair_other = shift(other, partner)

    owned = jnp.concatenate(
        (jnp.where(low_place, near, far), jnp.where(low_place, far, near)), axis=1
    ).astype(jnp.bfloat16)
    projected = gather(owned, fsdp)

    low = contract(activations, projected[:tokens], ((0,), (0,)))
    low += contract(act_pair, projected[tokens:], ((0,), (0,)))
    low = low.astype(jnp.bfloat16)
    low = summed(exchange(low.reshape(16, -1, 2 * ranks), rest))
    low = exchange(low.reshape(4, rows, 2 * ranks), "x")
    low_grad = jnp.concatenate((low[0] + low[3], low[1] + low[2]), axis=1)

    first_in = ranks_by_half(moment_one_in[0])
    second_in = ranks_by_half(moment_two_in[0])
    moment_one = decay_first * first_in + (1.0 - decay_first) * low_grad
    moment_two = decay_second * second_in + (1.0 - decay_second) * low_grad * low_grad
    direction = (bias_first * moment_one / (jnp.sqrt(bias_second * moment_two) + epsilon)).astype(
        jnp.bfloat16
    )
    direction, pair_other = lax.optimization_barrier((direction, pair_other))
    stacked = copies(direction, fsdp).reshape(blocks * rows, 4, ranks)

    def columns(owners):
        return lax.dynamic_index_in_dim(
            stacked, ((owners & 1) * 2) ^ ((owners >> 1) * 3), 1, keepdims=False
        )

    update = contract(columns(place), own, ((1,), (0,)))
    update += contract(columns(3 - place), other, ((1,), (0,)))
    update += contract(columns(place ^ 1), pair_own, ((1,), (0,)))
    update += contract(columns(place ^ 2), pair_other, ((1,), (0,)))
    updated = (weight.astype(jnp.float32) - step_scale * update.reshape(weight.shape)).astype(
        jnp.bfloat16
    )
    column = gather(updated[None], "zl")
    halves = [
        lax.all_gather(column[:, part * 4 : part * 4 + 4], "core", axis=1) for part in range(2)
    ]
    both = jnp.concatenate(halves, axis=2)
    new_weight = both.transpose(2, 3, 0, 1, 4).reshape(blocks, rows, 8 * ff_local)
    return (
        new_weight,
        ranks_in_order(moment_one)[None],
        ranks_in_order(moment_two)[None],
    )


def solution(mesh):
    fine = Mesh(mesh.devices.reshape(fine_sizes), fine_axes)
    in_specs = (
        P(dp, fsdp),
        P(dp, fsdp),
        P(dp, fsdp),
        P(None, dp, fsdp),
        P(fsdp, dp, None),
        P(fsdp, dp, None),
    )
    out_specs = (P(None, dp, None), P(fsdp, dp, None), P(fsdp, dp, None))
    return jax.shard_map(shards, mesh=fine, in_specs=in_specs, out_specs=out_specs, check_vma=False)
```

```python
import jax
import jax.numpy as jnp
from jax import lax
from jax.sharding import Mesh, PartitionSpec as P

decay_first = 0.9
decay_second = 0.95
bias_first = 1.0 / (1.0 - 0.9**10)
bias_second = 1.0 / (1.0 - 0.95**10)
step_scale = 0.25
epsilon = 1e-08

fine_axes = ("zh", "y", "x", "zl", "core")
fine_sizes = (2, 8, 4, 4, 2)
dp = ("zh", "y", "x")
rest = ("zh", "y")
fsdp = ("zl", "core")


def exchange(block, axes):
    return lax.all_to_all(block, axes, 0, 0, tiled=True)


def copies(block, axes):
    return exchange(jnp.broadcast_to(block[None], (lax.axis_size(axes),) + block.shape), axes)


def contract(left, right, dims):
    return lax.dot_general(left, right, (dims, ((), ())), preferred_element_type=jnp.float32)


def summed(pieces):
    return jnp.sum(pieces.astype(jnp.float32), axis=0)


def shift(block, pairs):
    return lax.ppermute(block, "x", [(i, j) for i, j in enumerate(pairs)])


def after(block, *others):
    return lax.optimization_barrier((block,) + others)[0]


partner = (1, 0, 3, 2)
mirror = (3, 2, 1, 0)
quarters = (0, 3, 1, 2)


def ranks_by_half(moment):
    rows, ranks = moment.shape
    parts = moment.reshape(rows, 2, 8, 4, 16).transpose(0, 3, 2, 1, 4)
    return jnp.concatenate([parts[:, q : q + 1] for q in quarters], axis=1).reshape(rows, ranks)


def ranks_in_order(moment):
    rows, ranks = moment.shape
    parts = moment.reshape(rows, 4, 8, 2, 16)
    parts = [parts[:, quarters.index(q)][:, None] for q in range(4)]
    return jnp.concatenate(parts, axis=1).transpose(0, 3, 2, 1, 4).reshape(rows, ranks)


def gather(block, axes):
    return lax.all_gather(block, axes, axis=0, tiled=True)


def shards(activations, grad_out, projector, weight, moment_one_in, moment_two_in):
    blocks, rows, ff_local = weight.shape
    rank_total = moment_one_in.shape[2]
    tokens, features = activations.shape
    groups = lax.axis_size(fsdp)
    place = lax.axis_index("x")
    low_place = place < 2

    grad_pair = shift(grad_out, partner)
    act_pair = shift(activations, partner)
    own = gather(gather(projector, "zh"), "y")
    other = shift(own, mirror)
    ranks = own.shape[0]

    def project(basis):
        parts = [
            contract(part, basis, ((1,), (1,))).astype(jnp.bfloat16)
            for part in (grad_out, grad_pair)
        ]
        return jnp.concatenate(parts).reshape(groups, -1, ranks)

    near = summed(exchange(project(own), fsdp))
    near, act_pair = lax.optimization_barrier((near, act_pair))
    far = summed(exchange(project(after(other, near)), fsdp))
    pair_own = shift(own, partner)
    pair_other = shift(other, partner)

    owned = jnp.concatenate(
        (jnp.where(low_place, near, far), jnp.where(low_place, far, near)), axis=1
    ).astype(jnp.bfloat16)
    projected = after(gather(owned, fsdp), pair_own)

    low = contract(activations, projected[:tokens], ((0,), (0,)))
    low += contract(act_pair, projected[tokens:], ((0,), (0,)))
    low = low.astype(jnp.bfloat16)
    low = summed(exchange(low.reshape(16, -1, 2 * ranks), rest))
    low = exchange(low.reshape(4, rows, 2 * ranks), "x")
    low_grad = jnp.concatenate((low[0] + low[3], low[1] + low[2]), axis=1)

    first_in = ranks_by_half(moment_one_in[0])
    second_in = ranks_by_half(moment_two_in[0])
    moment_one = decay_first * first_in + (1.0 - decay_first) * low_grad
    moment_two = decay_second * second_in + (1.0 - decay_second) * low_grad * low_grad
    direction = (bias_first * moment_one / (jnp.sqrt(bias_second * moment_two) + epsilon)).astype(
        jnp.bfloat16
    )
    stacked = copies(direction, fsdp).reshape(blocks * rows, 4, ranks)

    def columns(owners):
        return lax.dynamic_index_in_dim(
            stacked, ((owners & 1) * 2) ^ ((owners >> 1) * 3), 1, keepdims=False
        )

    update = contract(columns(place), own, ((1,), (0,)))
    update += contract(columns(3 - place), other, ((1,), (0,)))
    update += contract(columns(place ^ 1), pair_own, ((1,), (0,)))
    update += contract(columns(place ^ 2), pair_other, ((1,), (0,)))
    updated = (weight.astype(jnp.float32) - step_scale * update.reshape(weight.shape)).astype(
        jnp.bfloat16
    )
    column = gather(updated[None], "zl")
    halves = [
        lax.all_gather(column[:, part * 4 : part * 4 + 4], "core", axis=1) for part in range(2)
    ]
    both = jnp.concatenate(halves, axis=2).reshape(8, blocks, rows, ff_local)
    new_weight = both.transpose(1, 2, 0, 3).reshape(blocks, rows, 8 * ff_local)
    return (
        new_weight,
        ranks_in_order(moment_one)[None],
        ranks_in_order(moment_two)[None],
    )


def solution(mesh):
    fine = Mesh(mesh.devices.reshape(fine_sizes), fine_axes)
    in_specs = (
        P(dp, fsdp),
        P(dp, fsdp),
        P(dp, fsdp),
        P(None, dp, fsdp),
        P(fsdp, dp, None),
        P(fsdp, dp, None),
    )
    out_specs = (P(None, dp, None), P(fsdp, dp, None), P(fsdp, dp, None))
    return jax.shard_map(shards, mesh=fine, in_specs=in_specs, out_specs=out_specs, check_vma=False)
```

```python
import jax
import jax.numpy as jnp
from jax import lax
from jax.sharding import Mesh, PartitionSpec as P

decay_first = 0.9
decay_second = 0.95
bias_first = 1.0 / (1.0 - 0.9**10)
bias_second = 1.0 / (1.0 - 0.95**10)
step_scale = 0.25
epsilon = 1e-08

fine_axes = ("zh", "y", "x", "zl", "core")
fine_sizes = (2, 8, 4, 4, 2)
dp = ("zh", "y", "x")
rest = ("zh", "y")
fsdp = ("zl", "core")


def exchange(block, axes):
    return lax.all_to_all(block, axes, 0, 0, tiled=True)


def copies(block, axes):
    return exchange(jnp.broadcast_to(block[None], (lax.axis_size(axes),) + block.shape), axes)


def contract(left, right, dims):
    return lax.dot_general(left, right, (dims, ((), ())), preferred_element_type=jnp.float32)


def summed(pieces):
    return jnp.sum(pieces.astype(jnp.float32), axis=0)


def shift(block, pairs):
    return lax.ppermute(block, "x", [(i, j) for i, j in enumerate(pairs)])


def after(block, *others):
    return lax.optimization_barrier((block,) + others)[0]


partner = (1, 0, 3, 2)
mirror = (3, 2, 1, 0)
quarters = (0, 3, 1, 2)


def ranks_by_half(moment):
    rows, ranks = moment.shape
    parts = moment.reshape(rows, 2, 8, 4, 16).transpose(0, 3, 2, 1, 4)
    return jnp.concatenate([parts[:, q : q + 1] for q in quarters], axis=1).reshape(rows, ranks)


def ranks_in_order(moment):
    rows, ranks = moment.shape
    parts = moment.reshape(rows, 4, 8, 2, 16)
    parts = [parts[:, quarters.index(q)][:, None] for q in range(4)]
    return jnp.concatenate(parts, axis=1).transpose(0, 3, 2, 1, 4).reshape(rows, ranks)


def gather(block, axes):
    return lax.all_gather(block, axes, axis=0, tiled=True)


def shards(activations, grad_out, projector, weight, moment_one_in, moment_two_in):
    blocks, rows, ff_local = weight.shape
    rank_total = moment_one_in.shape[2]
    tokens, features = activations.shape
    groups = lax.axis_size(fsdp)
    place = lax.axis_index("x")
    low_place = place < 2

    grad_pair = shift(grad_out, partner)
    act_pair = shift(activations, partner)
    own = gather(gather(projector, "zh"), "y")
    other = shift(own, mirror)
    ranks = own.shape[0]

    def project(basis):
        parts = [
            contract(part, basis, ((1,), (1,))).astype(jnp.bfloat16)
            for part in (grad_out, grad_pair)
        ]
        return jnp.concatenate(parts).reshape(groups, -1, ranks)

    near, act_pair = lax.optimization_barrier((project(own), act_pair))
    near = summed(exchange(near, fsdp))
    far = summed(exchange(project(after(other, near)), fsdp))
    pair_own = shift(own, partner)
    pair_other = shift(other, partner)

    owned = jnp.concatenate(
        (jnp.where(low_place, near, far), jnp.where(low_place, far, near)), axis=1
    ).astype(jnp.bfloat16)
    projected = after(gather(owned, fsdp), pair_own)

    low = contract(activations, projected[:tokens], ((0,), (0,)))
    low += contract(act_pair, projected[tokens:], ((0,), (0,)))
    low = low.astype(jnp.bfloat16)
    low = summed(exchange(low.reshape(16, -1, 2 * ranks), rest))
    low = exchange(low.reshape(4, rows, 2 * ranks), "x")
    low_grad = jnp.concatenate((low[0] + low[3], low[1] + low[2]), axis=1)

    first_in = ranks_by_half(moment_one_in[0])
    second_in = ranks_by_half(moment_two_in[0])
    moment_one = decay_first * first_in + (1.0 - decay_first) * low_grad
    moment_two = decay_second * second_in + (1.0 - decay_second) * low_grad * low_grad
    direction = (bias_first * moment_one / (jnp.sqrt(bias_second * moment_two) + epsilon)).astype(
        jnp.bfloat16
    )
    stacked = copies(direction, fsdp).reshape(blocks * rows, 4, ranks)

    def columns(owners):
        return lax.dynamic_index_in_dim(
            stacked, ((owners & 1) * 2) ^ ((owners >> 1) * 3), 1, keepdims=False
        )

    update = contract(columns(place), own, ((1,), (0,)))
    update += contract(columns(3 - place), other, ((1,), (0,)))
    update += contract(columns(place ^ 1), pair_own, ((1,), (0,)))
    update += contract(columns(place ^ 2), pair_other, ((1,), (0,)))
    updated = (weight.astype(jnp.float32) - step_scale * update.reshape(weight.shape)).astype(
        jnp.bfloat16
    )
    column = gather(updated[None], "zl")
    halves = [
        lax.all_gather(column[:, part * 4 : part * 4 + 4], "core", axis=1) for part in range(2)
    ]
    both = jnp.concatenate(halves, axis=2).reshape(8, blocks, rows, ff_local)
    new_weight = both.transpose(1, 2, 0, 3).reshape(blocks, rows, 8 * ff_local)
    return (
        new_weight,
        ranks_in_order(moment_one)[None],
        ranks_in_order(moment_two)[None],
    )


def solution(mesh):
    fine = Mesh(mesh.devices.reshape(fine_sizes), fine_axes)
    in_specs = (
        P(dp, fsdp),
        P(dp, fsdp),
        P(dp, fsdp),
        P(None, dp, fsdp),
        P(fsdp, dp, None),
        P(fsdp, dp, None),
    )
    out_specs = (P(None, dp, None), P(fsdp, dp, None), P(fsdp, dp, None))
    return jax.shard_map(shards, mesh=fine, in_specs=in_specs, out_specs=out_specs, check_vma=False)
```

```python
import jax
import jax.numpy as jnp
from jax import lax
from jax.sharding import Mesh, PartitionSpec as P

decay_first = 0.9
decay_second = 0.95
bias_first = 1.0 / (1.0 - 0.9**10)
bias_second = 1.0 / (1.0 - 0.95**10)
step_scale = 0.25
epsilon = 1e-08

fine_axes = ("zh", "y", "x", "zl", "core")
fine_sizes = (2, 8, 4, 4, 2)
dp = ("zh", "y", "x")
rest = ("zh", "y")
fsdp = ("zl", "core")


def exchange(block, axes):
    return lax.all_to_all(block, axes, 0, 0, tiled=True)


def copies(block, axes):
    return exchange(jnp.broadcast_to(block[None], (lax.axis_size(axes),) + block.shape), axes)


def contract(left, right, dims):
    return lax.dot_general(left, right, (dims, ((), ())), preferred_element_type=jnp.float32)


def summed(pieces):
    return jnp.sum(pieces.astype(jnp.float32), axis=0)


def shift(block, pairs):
    return lax.ppermute(block, "x", [(i, j) for i, j in enumerate(pairs)])


def after(block, *others):
    return lax.optimization_barrier((block,) + others)[0]


partner = (1, 0, 3, 2)
mirror = (3, 2, 1, 0)
quarters = (0, 3, 1, 2)


def ranks_by_half(moment):
    rows, ranks = moment.shape
    parts = moment.reshape(rows, 2, 8, 4, 16).transpose(0, 3, 2, 1, 4)
    return jnp.concatenate([parts[:, q : q + 1] for q in quarters], axis=1).reshape(rows, ranks)


def ranks_in_order(moment):
    rows, ranks = moment.shape
    parts = moment.reshape(rows, 4, 8, 2, 16)
    parts = [parts[:, quarters.index(q)][:, None] for q in range(4)]
    return jnp.concatenate(parts, axis=1).transpose(0, 3, 2, 1, 4).reshape(rows, ranks)


def gather(block, axes):
    return lax.all_gather(block, axes, axis=0, tiled=True)


def shards(activations, grad_out, projector, weight, moment_one_in, moment_two_in):
    blocks, rows, ff_local = weight.shape
    rank_total = moment_one_in.shape[2]
    tokens, features = activations.shape
    groups = lax.axis_size(fsdp)
    place = lax.axis_index("x")
    low_place = place < 2

    grad_pair = shift(grad_out, partner)
    act_pair = shift(activations, partner)
    own = gather(gather(projector, "zh"), "y")
    other = shift(own, mirror)
    ranks = own.shape[0]

    def project(basis):
        parts = [
            contract(part, basis, ((1,), (1,))).astype(jnp.bfloat16)
            for part in (grad_out, grad_pair)
        ]
        return jnp.concatenate(parts).reshape(groups, -1, ranks)

    near = summed(exchange(project(own), fsdp))
    far = summed(exchange(project(after(other, near)), fsdp))
    pair_own = shift(own, partner)
    pair_other = shift(other, partner)

    owned = jnp.concatenate(
        (jnp.where(low_place, near, far), jnp.where(low_place, far, near)), axis=1
    ).astype(jnp.bfloat16)
    projected = gather(owned, fsdp)

    low = contract(activations, projected[:tokens], ((0,), (0,)))
    low += contract(act_pair, projected[tokens:], ((0,), (0,)))
    low = after(low.astype(jnp.bfloat16), pair_own)
    low = summed(exchange(low.reshape(16, -1, 2 * ranks), rest))
    low = exchange(low.reshape(4, rows, 2 * ranks), "x")
    low_grad = jnp.concatenate((low[0] + low[3], low[1] + low[2]), axis=1)

    first_in = ranks_by_half(moment_one_in[0])
    second_in = ranks_by_half(moment_two_in[0])
    moment_one = decay_first * first_in + (1.0 - decay_first) * low_grad
    moment_two = decay_second * second_in + (1.0 - decay_second) * low_grad * low_grad
    direction = (bias_first * moment_one / (jnp.sqrt(bias_second * moment_two) + epsilon)).astype(
        jnp.bfloat16
    )
    stacked = copies(direction, fsdp).reshape(blocks * rows, 4, ranks)

    def columns(owners):
        return lax.dynamic_index_in_dim(
            stacked, ((owners & 1) * 2) ^ ((owners >> 1) * 3), 1, keepdims=False
        )

    update = contract(columns(place), own, ((1,), (0,)))
    update += contract(columns(3 - place), other, ((1,), (0,)))
    update += contract(columns(place ^ 1), pair_own, ((1,), (0,)))
    update += contract(columns(place ^ 2), pair_other, ((1,), (0,)))
    updated = (weight.astype(jnp.float32) - step_scale * update.reshape(weight.shape)).astype(
        jnp.bfloat16
    )
    column = gather(updated[None], "zl")
    halves = [
        lax.all_gather(column[:, part * 4 : part * 4 + 4], "core", axis=1) for part in range(2)
    ]
    both = jnp.concatenate(halves, axis=2).reshape(8, blocks, rows, ff_local)
    new_weight = both.transpose(1, 2, 0, 3).reshape(blocks, rows, 8 * ff_local)
    return (
        new_weight,
        ranks_in_order(moment_one)[None],
        ranks_in_order(moment_two)[None],
    )


def solution(mesh):
    fine = Mesh(mesh.devices.reshape(fine_sizes), fine_axes)
    in_specs = (
        P(dp, fsdp),
        P(dp, fsdp),
        P(dp, fsdp),
        P(None, dp, fsdp),
        P(fsdp, dp, None),
        P(fsdp, dp, None),
    )
    out_specs = (P(None, dp, None), P(fsdp, dp, None), P(fsdp, dp, None))
    return jax.shard_map(shards, mesh=fine, in_specs=in_specs, out_specs=out_specs, check_vma=False)
```

```python
import jax
import jax.numpy as jnp
from jax import lax
from jax.sharding import Mesh, PartitionSpec as P

decay_first = 0.9
decay_second = 0.95
bias_first = 1.0 / (1.0 - 0.9**10)
bias_second = 1.0 / (1.0 - 0.95**10)
step_scale = 0.25
epsilon = 1e-08

fine_axes = ("zh", "y", "x", "zl", "core")
fine_sizes = (2, 8, 4, 4, 2)
dp = ("zh", "y", "x")
rest = ("zh", "y")
fsdp = ("zl", "core")


def exchange(block, axes):
    return lax.all_to_all(block, axes, 0, 0, tiled=True)


def copies(block, axes):
    return exchange(jnp.broadcast_to(block[None], (lax.axis_size(axes),) + block.shape), axes)


def contract(left, right, dims):
    return lax.dot_general(left, right, (dims, ((), ())), preferred_element_type=jnp.float32)


def summed(pieces):
    return jnp.sum(pieces.astype(jnp.float32), axis=0)


def shift(block, pairs):
    return lax.ppermute(block, "x", [(i, j) for i, j in enumerate(pairs)])


def after(block, *others):
    return lax.optimization_barrier((block,) + others)[0]


partner = (1, 0, 3, 2)
mirror = (3, 2, 1, 0)
quarters = (0, 3, 1, 2)


def ranks_by_half(moment):
    rows, ranks = moment.shape
    parts = moment.reshape(rows, 2, 8, 4, 16).transpose(0, 3, 2, 1, 4)
    return jnp.concatenate([parts[:, q : q + 1] for q in quarters], axis=1).reshape(rows, ranks)


def ranks_in_order(moment):
    rows, ranks = moment.shape
    parts = moment.reshape(rows, 4, 8, 2, 16)
    parts = [parts[:, quarters.index(q)][:, None] for q in range(4)]
    return jnp.concatenate(parts, axis=1).transpose(0, 3, 2, 1, 4).reshape(rows, ranks)


def gather(block, axes):
    return lax.all_gather(block, axes, axis=0, tiled=True)


def shards(activations, grad_out, projector, weight, moment_one_in, moment_two_in):
    blocks, rows, ff_local = weight.shape
    rank_total = moment_one_in.shape[2]
    tokens, features = activations.shape
    groups = lax.axis_size(fsdp)
    place = lax.axis_index("x")
    low_place = place < 2

    grad_pair = shift(grad_out, partner)
    act_pair = shift(activations, partner)
    own = gather(gather(projector, "zh"), "y")
    other = shift(own, mirror)
    ranks = own.shape[0]

    def project(basis):
        parts = [
            contract(part, basis, ((1,), (1,))).astype(jnp.bfloat16)
            for part in (grad_out, grad_pair)
        ]
        return jnp.concatenate(parts).reshape(groups, -1, ranks)

    near = summed(exchange(project(own), fsdp))
    far = summed(exchange(project(after(other, near)), fsdp))
    pair_own = shift(own, partner)
    pair_other = shift(other, partner)

    owned = jnp.concatenate(
        (jnp.where(low_place, near, far), jnp.where(low_place, far, near)), axis=1
    ).astype(jnp.bfloat16)
    projected = gather(after(owned, act_pair), fsdp)

    low = contract(activations, projected[:tokens], ((0,), (0,)))
    low += contract(act_pair, projected[tokens:], ((0,), (0,)))
    low = after(low.astype(jnp.bfloat16), pair_own)
    low = summed(exchange(low.reshape(16, -1, 2 * ranks), rest))
    low = exchange(low.reshape(4, rows, 2 * ranks), "x")
    low_grad = jnp.concatenate((low[0] + low[3], low[1] + low[2]), axis=1)

    first_in = ranks_by_half(moment_one_in[0])
    second_in = ranks_by_half(moment_two_in[0])
    moment_one = decay_first * first_in + (1.0 - decay_first) * low_grad
    moment_two = decay_second * second_in + (1.0 - decay_second) * low_grad * low_grad
    direction = (bias_first * moment_one / (jnp.sqrt(bias_second * moment_two) + epsilon)).astype(
        jnp.bfloat16
    )
    stacked = copies(direction, fsdp).reshape(blocks * rows, 4, ranks)

    def columns(owners):
        return lax.dynamic_index_in_dim(
            stacked, ((owners & 1) * 2) ^ ((owners >> 1) * 3), 1, keepdims=False
        )

    update = contract(columns(place), own, ((1,), (0,)))
    update += contract(columns(3 - place), other, ((1,), (0,)))
    update += contract(columns(place ^ 1), pair_own, ((1,), (0,)))
    update += contract(columns(place ^ 2), pair_other, ((1,), (0,)))
    updated = (weight.astype(jnp.float32) - step_scale * update.reshape(weight.shape)).astype(
        jnp.bfloat16
    )
    column = gather(updated[None], "zl")
    halves = [
        lax.all_gather(column[:, part * 4 : part * 4 + 4], "core", axis=1) for part in range(2)
    ]
    both = jnp.concatenate(halves, axis=2).reshape(8, blocks, rows, ff_local)
    new_weight = both.transpose(1, 2, 0, 3).reshape(blocks, rows, 8 * ff_local)
    return (
        new_weight,
        ranks_in_order(moment_one)[None],
        ranks_in_order(moment_two)[None],
    )


def solution(mesh):
    fine = Mesh(mesh.devices.reshape(fine_sizes), fine_axes)
    in_specs = (
        P(dp, fsdp),
        P(dp, fsdp),
        P(dp, fsdp),
        P(None, dp, fsdp),
        P(fsdp, dp, None),
        P(fsdp, dp, None),
    )
    out_specs = (P(None, dp, None), P(fsdp, dp, None), P(fsdp, dp, None))
    return jax.shard_map(shards, mesh=fine, in_specs=in_specs, out_specs=out_specs, check_vma=False)
```

```python
import jax
import jax.numpy as jnp
from jax import lax
from jax.sharding import Mesh, PartitionSpec as P

decay_first = 0.9
decay_second = 0.95
bias_first = 1.0 / (1.0 - 0.9**10)
bias_second = 1.0 / (1.0 - 0.95**10)
step_scale = 0.25
epsilon = 1e-08

fine_axes = ("zh", "y", "x", "zl", "core")
fine_sizes = (2, 8, 4, 4, 2)
dp = ("zh", "y", "x")
rest = ("zh", "y")
fsdp = ("zl", "core")


def exchange(block, axes):
    return lax.all_to_all(block, axes, 0, 0, tiled=True)


def copies(block, axes):
    return exchange(jnp.broadcast_to(block[None], (lax.axis_size(axes),) + block.shape), axes)


def contract(left, right, dims):
    return lax.dot_general(left, right, (dims, ((), ())), preferred_element_type=jnp.float32)


def summed(pieces):
    return jnp.sum(pieces.astype(jnp.float32), axis=0)


def shift(block, pairs):
    return lax.ppermute(block, "x", [(i, j) for i, j in enumerate(pairs)])


def after(block, *others):
    return lax.optimization_barrier((block,) + others)[0]


partner = (1, 0, 3, 2)
mirror = (3, 2, 1, 0)
quarters = (0, 3, 1, 2)


def ranks_by_half(moment):
    rows, ranks = moment.shape
    parts = moment.reshape(rows, 2, 8, 4, 16).transpose(0, 3, 2, 1, 4)
    return jnp.concatenate([parts[:, q : q + 1] for q in quarters], axis=1).reshape(rows, ranks)


def ranks_in_order(moment):
    rows, ranks = moment.shape
    parts = moment.reshape(rows, 4, 8, 2, 16)
    parts = [parts[:, quarters.index(q)][:, None] for q in range(4)]
    return jnp.concatenate(parts, axis=1).transpose(0, 3, 2, 1, 4).reshape(rows, ranks)


def gather(block, axes):
    return lax.all_gather(block, axes, axis=0, tiled=True)


def shards(activations, grad_out, projector, weight, moment_one_in, moment_two_in):
    blocks, rows, ff_local = weight.shape
    rank_total = moment_one_in.shape[2]
    tokens, features = activations.shape
    groups = lax.axis_size(fsdp)
    place = lax.axis_index("x")
    low_place = place < 2

    grad_pair = shift(grad_out, partner)
    act_pair = shift(activations, partner)
    own = gather(gather(projector, "zh"), "y")
    other = shift(own, mirror)
    ranks = own.shape[0]

    def project(basis):
        parts = [
            contract(part, basis, ((1,), (1,))).astype(jnp.bfloat16)
            for part in (grad_out, grad_pair)
        ]
        return jnp.concatenate(parts).reshape(groups, -1, ranks)

    near = summed(exchange(project(own), fsdp))
    far = summed(exchange(project(after(other, near)), fsdp))
    pair_own = shift(after(own, act_pair), partner)
    pair_other = shift(other, partner)

    owned = jnp.concatenate(
        (jnp.where(low_place, near, far), jnp.where(low_place, far, near)), axis=1
    ).astype(jnp.bfloat16)
    projected = gather(owned, fsdp)

    low = contract(activations, projected[:tokens], ((0,), (0,)))
    low += contract(act_pair, projected[tokens:], ((0,), (0,)))
    low = after(low.astype(jnp.bfloat16), pair_own)
    low = summed(exchange(low.reshape(16, -1, 2 * ranks), rest))
    low = exchange(low.reshape(4, rows, 2 * ranks), "x")
    low_grad = jnp.concatenate((low[0] + low[3], low[1] + low[2]), axis=1)

    first_in = ranks_by_half(moment_one_in[0])
    second_in = ranks_by_half(moment_two_in[0])
    moment_one = decay_first * first_in + (1.0 - decay_first) * low_grad
    moment_two = decay_second * second_in + (1.0 - decay_second) * low_grad * low_grad
    direction = (bias_first * moment_one / (jnp.sqrt(bias_second * moment_two) + epsilon)).astype(
        jnp.bfloat16
    )
    stacked = copies(direction, fsdp).reshape(blocks * rows, 4, ranks)

    def columns(owners):
        return lax.dynamic_index_in_dim(
            stacked, ((owners & 1) * 2) ^ ((owners >> 1) * 3), 1, keepdims=False
        )

    update = contract(columns(place), own, ((1,), (0,)))
    update += contract(columns(3 - place), other, ((1,), (0,)))
    update += contract(columns(place ^ 1), pair_own, ((1,), (0,)))
    update += contract(columns(place ^ 2), pair_other, ((1,), (0,)))
    updated = (weight.astype(jnp.float32) - step_scale * update.reshape(weight.shape)).astype(
        jnp.bfloat16
    )
    column = gather(updated[None], "zl")
    halves = [
        lax.all_gather(column[:, part * 4 : part * 4 + 4], "core", axis=1) for part in range(2)
    ]
    both = jnp.concatenate(halves, axis=2).reshape(8, blocks, rows, ff_local)
    new_weight = both.transpose(1, 2, 0, 3).reshape(blocks, rows, 8 * ff_local)
    return (
        new_weight,
        ranks_in_order(moment_one)[None],
        ranks_in_order(moment_two)[None],
    )


def solution(mesh):
    fine = Mesh(mesh.devices.reshape(fine_sizes), fine_axes)
    in_specs = (
        P(dp, fsdp),
        P(dp, fsdp),
        P(dp, fsdp),
        P(None, dp, fsdp),
        P(fsdp, dp, None),
        P(fsdp, dp, None),
    )
    out_specs = (P(None, dp, None), P(fsdp, dp, None), P(fsdp, dp, None))
    return jax.shard_map(shards, mesh=fine, in_specs=in_specs, out_specs=out_specs, check_vma=False)
```
